512 devices in a mesh: node: 32 (over y_hi, z), tp: 16 (over x, y_lo, core).
Axes of the slice: x: 4, y: 4 (y_hi: 2, y_lo: 2; y = y_hi * 2 + y_lo), z: 16, core: 2. Of those that a mesh axis runs over, the one named last changes fastest.
Arguments:
- weights: bfloat16 [32, 6912, 2560], P('node', 'tp'), may hold values from -6 to 6
- hidden: bfloat16 [32, 384, 6912], P('node', None, 'tp'), may hold values from -6 to 6
- cotangent: bfloat16 [32, 384, 2560], P('node', 'tp'), may hold values from -6 to 6
- hop_index: int32 [1], replicated, may hold values from 0 to 2
Outputs:
- layer_out: bfloat16 [32, 384, 2560], P('node', 'tp')
- new_weights: bfloat16 [32, 6912, 2560], P('node', 'tp')
The draws below stay inside these ranges and needn't reach their ends.
Inputs may be any that keep to these rules, and one draw needn't show every extreme that they name: Node i averages with node i XOR 2^hop_index.
All inputs are finite; a program needn't handle non-finite values.
Results may differ from the reference program's by a relative error of at most 0.001.
Values may be sent and summed in bfloat16 or wider, within the bound.
No kernel may reach another device: no remote copies, remote signals or barrier semaphores. Data moves between devices by JAX's collectives and lax.ppermute only.
A program may use at most 64 MiB of HBM per device.

```python
import jax
import jax.numpy as jnp
from jax import lax

D = 2560
FF = 6912
TOK = 384
NODES = 32


def raised(drawn, stream_key, source, target, parts, factor):
    owner, partner = [(jnp.arange(drawn.shape[axis_at]) // (drawn.shape[axis_at] // parts)).reshape([-1 if axis == axis_at else 1 for axis in range(drawn.ndim)]) for axis_at in (source, target)]
    chosen = jax.random.permutation(stream_key, parts)[partner]
    strong = (owner == chosen) | (owner == (partner + parts // 2) % parts)
    return jnp.where(strong, factor * drawn, drawn)


def level_of(own_key, extent, split, smallest, high):
    factor_of, own = 1.0, jax.random.fold_in(own_key, 6)
    for dim, shards_of in split:
        steps = jnp.exp(jax.random.uniform(jax.random.fold_in(own, dim), (shards_of,), jnp.float32, smallest / len(split), high / len(split)))
        factor_of = factor_of * jnp.repeat(steps, extent[dim] // shards_of).reshape([-1 if axis == dim else 1 for axis in range(len(extent))])
    return factor_of


def noise(stream_key, dims, width, limit, pieces=(), kind=jnp.bfloat16):
    loudness = level_of(stream_key, dims, pieces, -0.22, 0.18) if pieces else 1.0
    values = jax.random.normal(stream_key, dims, jnp.float32) * width * loudness
    return jnp.minimum(jnp.maximum(values, -limit), limit).astype(kind)


def gaussian_with(stream_key, dims, spread, limit, cuts, heavy, held_as=jnp.bfloat16):
    array = spread * jax.random.normal(stream_key, dims, jnp.float32)
    if cuts:
        array = array * level_of(stream_key, dims, cuts, -0.22, 0.18)
    return jnp.clip(raised(array, jax.random.fold_in(stream_key, 3), *heavy), -limit, limit).astype(held_as)


def setup_inputs(seed: int = 0) -> dict:
    key_of = jax.random.split(jax.random.key(seed), 5)
    weights = noise(key_of[0], (NODES, FF, D), 1.0, 6.0, ((0, 32), (1, 16)))
    hidden = gaussian_with(key_of[1], (NODES, TOK, FF), 1.0, 6.0, ((0, 32), (2, 16)), (2, 1, 16, 2.0))
    cotangent = noise(key_of[2], (NODES, TOK, D), 1.0, 6.0, ((0, 32), (1, 16)))
    hop_index = jax.random.randint(key_of[3], (1,), 0, 3).astype(jnp.int32)
    return dict(weights=weights, hidden=hidden, cotangent=cotangent, hop_index=hop_index)


step_rate = 0.5


def panel_forward(operands):
    node_hidden, node_weights = operands
    multiplier = FF ** -0.5
    product = jnp.dot(node_hidden, node_weights, preferred_element_type=jnp.float32) * multiplier
    return product.astype(jnp.bfloat16)


def node_update(weights, hidden, cotangent, node_id):
    node_hidden = lax.dynamic_index_in_dim(hidden, node_id, 0, keepdims=False)
    node_cotan = lax.dynamic_index_in_dim(cotangent, node_id, 0, keepdims=False)
    node_weights = lax.dynamic_index_in_dim(weights, node_id, 0, keepdims=False)
    gradient = jnp.dot(node_hidden.T, node_cotan, preferred_element_type=jnp.float32) * (FF ** -0.5)
    return node_weights.astype(jnp.float32) - step_rate * gradient


def reference(weights, hidden, cotangent, hop_index):
    layer_out = lax.map(panel_forward, (hidden, weights))
    distance = jnp.left_shift(jnp.int32(1), hop_index[0].astype(jnp.int32))

    def pair_step(out_weights, pair_index):
        lower = pair_index % distance
        first_node = ((pair_index - lower) * 2 + lower).astype(jnp.int32)
        second_node = (first_node + distance).astype(jnp.int32)
        stepped_first = node_update(weights, hidden, cotangent, first_node)
        stepped_second = node_update(weights, hidden, cotangent, second_node)
        mean_stepped = ((stepped_first + stepped_second) * 0.5).astype(jnp.bfloat16)
        out_weights = lax.dynamic_update_index_in_dim(out_weights, mean_stepped, first_node, 0)
        out_weights = lax.dynamic_update_index_in_dim(out_weights, mean_stepped, second_node, 0)
        return out_weights, None

    pair_ids = jnp.arange(NODES // 2, dtype=jnp.int32)
    final_weights, unused_rest = lax.scan(pair_step, jnp.zeros_like(weights), pair_ids)
    return layer_out, final_weights
```

```python
from functools import partial

import jax
import jax.numpy as jnp
from jax import lax
from jax.sharding import PartitionSpec as P

FF = 6912
STEP_RATE = 0.5
HOP_LEVELS = 3
SCALE = FF ** (-0.5)
CHUNKS = (168, 168, 96)


def trade(value, level):
    pairs = [(i, i ^ 1 << level) for i in range(lax.axis_size("node"))]
    return lax.ppermute(value, "node", pairs)


def step(level, weights, hidden, cotangent):
    tokens, rows = hidden.shape
    shard, width = cotangent.shape
    groups = tokens // shard
    far_cotangent = trade(cotangent, level)
    flipped = hidden.T
    far_flipped = trade(flipped, level)
    far_weights, first = [], 0
    for size in CHUNKS:
        far_weights.append(trade(weights[first : first + size], level))
        first += size
    both = lax.all_gather(
        jnp.concatenate([cotangent, far_cotangent], 0), "tp", axis=0, tiled=True
    )
    layer_out = lax.psum_scatter(
        jnp.dot(hidden, weights, preferred_element_type=jnp.float32) * SCALE,
        "tp",
        scatter_dimension=0,
        tiled=True,
    ).astype(jnp.bfloat16)
    paired = jnp.stack(
        [
            flipped.reshape(rows, groups, shard),
            far_flipped.reshape(rows, groups, shard),
        ],
        2,
    ).reshape(rows, 2 * tokens)
    means, first = [], 0
    for size, far in zip(CHUNKS, far_weights):
        here = slice(first, first + size)
        gradient = jnp.dot(paired[here], both, preferred_element_type=jnp.float32)
        total = weights[here].astype(jnp.float32) + far.astype(jnp.float32)
        means.append((0.5 * total - (0.5 * STEP_RATE * SCALE) * gradient).astype(jnp.bfloat16))
        first += size
    return layer_out, jnp.concatenate(means, 0)


def per_device(weights, hidden, cotangent, hop_index):
    branches = [partial(step, level) for level in range(HOP_LEVELS)]
    layer_out, new_weights = lax.switch(
        hop_index[0], branches, weights[0], hidden[0], cotangent[0]
    )
    return layer_out[None], new_weights[None]


def solution(mesh):
    placed = (P("node", "tp", None), P("node", None, "tp"), P("node", "tp", None), P())
    return jax.shard_map(
        per_device,
        mesh=mesh,
        in_specs=placed,
        out_specs=(P("node", "tp", None), P("node", "tp", None)),
        check_vma=False,
    )
```

```python
from functools import partial

import jax
import jax.numpy as jnp
from jax import lax
from jax.experimental import pallas as pl
from jax.sharding import PartitionSpec as P

FF = 6912
STEP_RATE = 0.5
HOP_LEVELS = 3
SCALE = FF ** (-0.5)
CORES = 2
PLANS = {1: (112, (56, 56, 48), 1), 2: (0, (56, 56, 56, 48), 2)}


def after(value, *others):
    return lax.optimization_barrier((value, *others))[0]


def trade(value, level):
    pairs = [(i, i ^ 1 << level) for i in range(lax.axis_size("node"))]
    return lax.ppermute(value, "node", pairs)


def swap_cores(value):
    return lax.ppermute(value, "tp", [(i, i ^ 1) for i in range(lax.axis_size("tp"))])


def between_chips(blocks):
    chips = blocks.shape[0]
    same_core = [[CORES * i + j for i in range(chips)] for j in range(CORES)]
    return lax.all_to_all(blocks, "tp", 0, 0, axis_index_groups=same_core, tiled=True)


def chip_output(weights, hidden):
    tokens, rows = hidden.shape
    members = lax.axis_size("tp")
    chips, shard = members // CORES, tokens // members
    core = lax.rem(lax.axis_index("tp"), CORES)
    panel = hidden.reshape(chips, CORES, shard, rows)

    def partial_of(owner):
        chosen = lax.dynamic_index_in_dim(panel, owner, 1, keepdims=False)
        return SCALE * jnp.dot(
            chosen.reshape(chips * shard, rows), weights, preferred_element_type=jnp.float32
        )

    far = swap_cores(partial_of(1 - core))
    return (partial_of(core) + far).reshape(chips, shard, -1)


def interleave(near, far, members):
    rows, tokens = near.shape
    blocks = (rows, members, tokens // members)
    return jnp.stack([near.reshape(blocks), far.reshape(blocks)], 2).reshape(rows, 2 * tokens)


def arrived(value, *others, ahead=10**12):
    return pl.pallas_call(
        lambda *refs: None,
        in_specs=[pl.BlockSpec(memory_space=pl.ANY)] * (1 + len(others)),
        out_specs=pl.BlockSpec(memory_space=pl.ANY),
        out_shape=jax.ShapeDtypeStruct(value.shape, value.dtype),
        input_output_aliases={0: 0},
        cost_estimate=pl.CostEstimate(flops=ahead, bytes_accessed=0, transcendentals=0),
    )(value, *others)


def averaged(near, far, gradient):
    total = near.astype(jnp.float32) + far.astype(jnp.float32)
    return (0.5 * total - (0.5 * STEP_RATE * SCALE) * gradient).astype(jnp.bfloat16)


def pieces_of(sizes):
    first = 0
    for size in sizes:
        yield first, size
        first += size


def whole_step(level, weights, hidden, cotangent):
    tokens, rows = hidden.shape
    members = lax.axis_size("tp")
    far_cotangent = trade(cotangent, level)
    far_hidden = trade(hidden, level)
    far_weights = trade(weights, level)
    shards = jnp.concatenate([cotangent, far_cotangent], 0)
    both = lax.all_gather(shards, "tp", axis=0, tiled=True)
    chip_sum = chip_output(weights, hidden)
    layer_out = between_chips(chip_sum).sum(0).astype(jnp.bfloat16)
    both = arrived(both, far_weights, layer_out, ahead=0)
    blocks = (members, tokens // members, rows)
    panel = jnp.stack([hidden.reshape(blocks), far_hidden.reshape(blocks)], 1)
    gradient = lax.dot_general(
        panel.reshape(2 * tokens, rows),
        both,
        (((0,), (0,)), ((), ())),
        preferred_element_type=jnp.float32,
    )
    return layer_out, averaged(weights, far_weights, gradient)


def mixed_step(level, weights, hidden, cotangent):
    members = lax.axis_size("tp")
    shared, pieces, forward_by = PLANS[level]
    half = (weights.shape[0] - shared) // 2
    upper = (lax.axis_index("node") >> level) & 1
    mine, other = shared + half * upper, shared + half * (1 - upper)
    far_cotangent = trade(cotangent, level)
    shards = jnp.concatenate([cotangent, far_cotangent], 0)
    flipped = hidden.T

    def with_shared(first):
        if not shared:
            return lax.dynamic_slice_in_dim(flipped, first, half, 0)
        return jnp.concatenate(
            [flipped[:shared], lax.dynamic_slice_in_dim(flipped, first, half, 0)], 0
        )

    far_flipped = trade(after(with_shared(other), shards), level)
    far_weights = [
        trade(after(lax.dynamic_slice_in_dim(weights, other + a, n, 0), shards), level)
        for a, n in pieces_of(pieces)
    ]
    if shared:
        far_shared = trade(after(weights[:shared], shards), level)
    both = lax.all_gather(shards, "tp", axis=0, tiled=True)
    chip_sum = chip_output(weights, after(hidden, both))
    layer_out = between_chips(chip_sum).sum(0).astype(jnp.bfloat16)
    paired = interleave(with_shared(mine), far_flipped, members)
    gradient = jnp.dot(paired, both, preferred_element_type=jnp.float32)
    new_weights = jnp.zeros_like(weights)
    returned, order = [], []
    for k, ((a, n), far) in enumerate(zip(pieces_of(pieces), far_weights)):
        if k == forward_by:
            order.append(chip_sum)
        near = lax.dynamic_slice_in_dim(weights, mine + a, n, 0)
        mean = averaged(near, arrived(far, *order), gradient[shared + a : shared + a + n])
        order = [mean]
        returned.append(trade(mean, level))
        new_weights = lax.dynamic_update_slice_in_dim(new_weights, mean, mine + a, 0)
    if shared:
        far_shared = arrived(far_shared, *order)
        mean = averaged(weights[:shared], far_shared, gradient[:shared])
        new_weights = lax.dynamic_update_slice_in_dim(new_weights, mean, 0, 0)
    returned[-1] = arrived(returned[-1], layer_out, ahead=0)
    for (a, n), mean in zip(pieces_of(pieces), returned):
        new_weights = lax.dynamic_update_slice_in_dim(new_weights, mean, other + a, 0)
    return layer_out, new_weights


def per_device(weights, hidden, cotangent, hop_index):
    branches = [
        partial(mixed_step if level in PLANS else whole_step, level) for level in range(HOP_LEVELS)
    ]
    layer_out, new_weights = lax.switch(
        hop_index[0], branches, weights[0], hidden[0], cotangent[0]
    )
    return layer_out[None], new_weights[None]


def solution(mesh):
    placed = (P("node", "tp", None), P("node", None, "tp"), P("node", "tp", None), P())
    return jax.shard_map(
        per_device,
        mesh=mesh,
        in_specs=placed,
        out_specs=(P("node", "tp", None), P("node", "tp", None)),
        check_vma=False,
    )
```

```python
from functools import partial

import jax
import jax.numpy as jnp
from jax import lax
from jax.experimental import pallas as pl
from jax.sharding import PartitionSpec as P

FF = 6912
STEP_RATE = 0.5
HOP_LEVELS = 3
SCALE = FF ** (-0.5)
CORES = 2
PLANS = {1: (112, (56, 56, 48), 1), 2: (48, (56, 48, 48, 40), 2)}


def after(value, *others):
    return lax.optimization_barrier((value, *others))[0]


def trade(value, level):
    pairs = [(i, i ^ 1 << level) for i in range(lax.axis_size("node"))]
    return lax.ppermute(value, "node", pairs)


def swap_cores(value):
    return lax.ppermute(value, "tp", [(i, i ^ 1) for i in range(lax.axis_size("tp"))])


def between_chips(blocks):
    chips = blocks.shape[0]
    same_core = [[CORES * i + j for i in range(chips)] for j in range(CORES)]
    return lax.all_to_all(blocks, "tp", 0, 0, axis_index_groups=same_core, tiled=True)


def chip_output(weights, hidden):
    tokens, rows = hidden.shape
    members = lax.axis_size("tp")
    chips, shard = members // CORES, tokens // members
    core = lax.rem(lax.axis_index("tp"), CORES)
    panel = hidden.reshape(chips, CORES, shard, rows)

    def partial_of(owner):
        chosen = lax.dynamic_index_in_dim(panel, owner, 1, keepdims=False)
        return SCALE * jnp.dot(
            chosen.reshape(chips * shard, rows), weights, preferred_element_type=jnp.float32
        )

    far = swap_cores(partial_of(1 - core))
    return (partial_of(core) + far).reshape(chips, shard, -1)


def interleave(near, far, members):
    rows, tokens = near.shape
    blocks = (rows, members, tokens // members)
    return jnp.stack([near.reshape(blocks), far.reshape(blocks)], 2).reshape(rows, 2 * tokens)


def arrived(value, *others, ahead=10**12):
    return pl.pallas_call(
        lambda *refs: None,
        in_specs=[pl.BlockSpec(memory_space=pl.ANY)] * (1 + len(others)),
        out_specs=pl.BlockSpec(memory_space=pl.ANY),
        out_shape=jax.ShapeDtypeStruct(value.shape, value.dtype),
        input_output_aliases={0: 0},
        cost_estimate=pl.CostEstimate(flops=ahead, bytes_accessed=0, transcendentals=0),
    )(value, *others)


def averaged(near, far, gradient):
    total = near.astype(jnp.float32) + far.astype(jnp.float32)
    return (0.5 * total - (0.5 * STEP_RATE * SCALE) * gradient).astype(jnp.bfloat16)


def pieces_of(sizes):
    first = 0
    for size in sizes:
        yield first, size
        first += size


def whole_step(level, weights, hidden, cotangent):
    tokens, rows = hidden.shape
    members = lax.axis_size("tp")
    far_cotangent = trade(cotangent, level)
    far_hidden = trade(hidden, level)
    far_weights = trade(weights, level)
    shards = jnp.concatenate([cotangent, far_cotangent], 0)
    both = lax.all_gather(shards, "tp", axis=0, tiled=True)
    chip_sum = chip_output(weights, hidden)
    layer_out = between_chips(chip_sum).sum(0).astype(jnp.bfloat16)
    both = arrived(both, far_weights, layer_out, ahead=0)
    blocks = (members, tokens // members, rows)
    panel = jnp.stack([hidden.reshape(blocks), far_hidden.reshape(blocks)], 1)
    gradient = lax.dot_general(
        panel.reshape(2 * tokens, rows),
        both,
        (((0,), (0,)), ((), ())),
        preferred_element_type=jnp.float32,
    )
    return layer_out, averaged(weights, far_weights, gradient)


def mixed_step(level, weights, hidden, cotangent):
    members = lax.axis_size("tp")
    shared, pieces, forward_by = PLANS[level]
    half = (weights.shape[0] - shared) // 2
    upper = (lax.axis_index("node") >> level) & 1
    mine, other = shared + half * upper, shared + half * (1 - upper)
    far_cotangent = trade(cotangent, level)
    shards = jnp.concatenate([cotangent, far_cotangent], 0)
    flipped = hidden.T

    def with_shared(first):
        if not shared:
            return lax.dynamic_slice_in_dim(flipped, first, half, 0)
        return jnp.concatenate(
            [flipped[:shared], lax.dynamic_slice_in_dim(flipped, first, half, 0)], 0
        )

    late_weights = after(weights, shards) if level > 1 else weights
    sent = with_shared(other)
    far_flipped = trade(after(sent, shards) if level > 1 else sent, level)
    far_weights = [
        trade(after(lax.dynamic_slice_in_dim(late_weights, other + a, n, 0), shards), level)
        for a, n in pieces_of(pieces)
    ]
    if shared:
        far_shared = trade(after(late_weights[:shared], shards), level)
    both = lax.all_gather(shards, "tp", axis=0, tiled=True)
    chip_sum = chip_output(weights, after(hidden, both))
    layer_out = between_chips(chip_sum).sum(0).astype(jnp.bfloat16)
    paired = interleave(with_shared(mine), far_flipped, members)
    gradient = jnp.dot(paired, both, preferred_element_type=jnp.float32)
    new_weights = arrived(jnp.zeros_like(weights), shards, ahead=0)
    returned, order = [], []
    for k, ((a, n), far) in enumerate(zip(pieces_of(pieces), far_weights)):
        if k == forward_by:
            order.append(chip_sum)
        near = lax.dynamic_slice_in_dim(weights, mine + a, n, 0)
        mean = averaged(near, arrived(far, *order), gradient[shared + a : shared + a + n])
        order = [mean]
        returned.append(trade(mean, level))
        new_weights = lax.dynamic_update_slice_in_dim(new_weights, mean, mine + a, 0)
    if shared:
        far_shared = arrived(far_shared, *order)
        mean = averaged(weights[:shared], far_shared, gradient[:shared])
        new_weights = lax.dynamic_update_slice_in_dim(new_weights, mean, 0, 0)
    returned[-1] = arrived(returned[-1], layer_out, ahead=0)
    for (a, n), mean in zip(pieces_of(pieces), returned):
        new_weights = lax.dynamic_update_slice_in_dim(new_weights, mean, other + a, 0)
    return layer_out, new_weights


def per_device(weights, hidden, cotangent, hop_index):
    branches = [
        partial(mixed_step if level in PLANS else whole_step, level) for level in range(HOP_LEVELS)
    ]
    layer_out, new_weights = lax.switch(
        hop_index[0], branches, weights[0], hidden[0], cotangent[0]
    )
    return layer_out[None], new_weights[None]


def solution(mesh):
    placed = (P("node", "tp", None), P("node", None, "tp"), P("node", "tp", None), P())
    return jax.shard_map(
        per_device,
        mesh=mesh,
        in_specs=placed,
        out_specs=(P("node", "tp", None), P("node", "tp", None)),
        check_vma=False,
    )
```

```python
from functools import partial

import jax
import jax.numpy as jnp
from jax import lax
from jax.experimental import pallas as pl
from jax.experimental.layout import Layout, with_layout_constraint
from jax.sharding import PartitionSpec as P

FF = 6912
STEP_RATE = 0.5
HOP_LEVELS = 3
SCALE = FF ** (-0.5)
CORES = 2
PLANS = {1: (112, (48, 56, 56), 1), 2: (48, (56, 48, 48, 40), 2)}


def after(value, *others):
    return lax.optimization_barrier((value, *others))[0]


def trade(value, level):
    pairs = [(i, i ^ 1 << level) for i in range(lax.axis_size("node"))]
    return lax.ppermute(value, "node", pairs)


def swap_cores(value):
    return lax.ppermute(value, "tp", [(i, i ^ 1) for i in range(lax.axis_size("tp"))])


def between_chips(blocks):
    chips = blocks.shape[0]
    same_core = [[CORES * i + j for i in range(chips)] for j in range(CORES)]
    return lax.all_to_all(blocks, "tp", 0, 0, axis_index_groups=same_core, tiled=True)


def chip_output(weights, hidden):
    tokens, rows = hidden.shape
    members = lax.axis_size("tp")
    chips, shard = members // CORES, tokens // members
    core = lax.rem(lax.axis_index("tp"), CORES)
    panel = hidden.reshape(chips, CORES, shard, rows)

    def partial_of(owner):
        chosen = lax.dynamic_index_in_dim(panel, owner, 1, keepdims=False)
        return SCALE * jnp.dot(
            chosen.reshape(chips * shard, rows), weights, preferred_element_type=jnp.float32
        )

    far = swap_cores(partial_of(1 - core))
    return (partial_of(core) + far).reshape(chips, shard, -1)


def interleave(near, far, members):
    rows, tokens = near.shape
    blocks = (rows, members, tokens // members)
    return jnp.stack([near.reshape(blocks), far.reshape(blocks)], 2).reshape(rows, 2 * tokens)


def arrived(value, *others, ahead=10**12):
    return pl.pallas_call(
        lambda *refs: None,
        in_specs=[pl.BlockSpec(memory_space=pl.ANY)] * (1 + len(others)),
        out_specs=pl.BlockSpec(memory_space=pl.ANY),
        out_shape=jax.ShapeDtypeStruct(value.shape, value.dtype),
        input_output_aliases={0: 0},
        cost_estimate=pl.CostEstimate(flops=ahead, bytes_accessed=0, transcendentals=0),
    )(value, *others)


def averaged(near, far, gradient):
    total = near.astype(jnp.float32) + far.astype(jnp.float32)
    return (0.5 * total - (0.5 * STEP_RATE * SCALE) * gradient).astype(jnp.bfloat16)


def pieces_of(sizes):
    first = 0
    for size in sizes:
        yield first, size
        first += size


def whole_step(level, weights, hidden, cotangent):
    tokens, rows = hidden.shape
    members = lax.axis_size("tp")
    far_cotangent = trade(cotangent, level)
    far_hidden = trade(hidden, level)
    shards = jnp.concatenate([cotangent, far_cotangent], 0)
    both = lax.all_gather(shards, "tp", axis=0, tiled=True)
    chip_sum = chip_output(weights, hidden)
    far_weights = trade(weights, level)
    chip_sum = arrived(chip_sum)
    layer_out = between_chips(chip_sum).sum(0).astype(jnp.bfloat16)
    both = arrived(both, far_weights, layer_out, ahead=0)
    blocks = (members, tokens // members, rows)
    panel = jnp.stack([hidden.reshape(blocks), far_hidden.reshape(blocks)], 1)
    gradient = lax.dot_general(
        panel.reshape(2 * tokens, rows),
        both,
        (((0,), (0,)), ((), ())),
        preferred_element_type=jnp.float32,
    )
    return layer_out, averaged(weights, far_weights, gradient)


def mixed_step(level, weights, hidden, cotangent):
    members = lax.axis_size("tp")
    shared, pieces, forward_by = PLANS[level]
    half = (weights.shape[0] - shared) // 2
    upper = (lax.axis_index("node") >> level) & 1
    mine, other = shared + half * upper, shared + half * (1 - upper)
    far_cotangent = trade(cotangent, level)
    shards = jnp.concatenate([cotangent, far_cotangent], 0)
    flipped = hidden.T

    def with_shared(first):
        if not shared:
            return lax.dynamic_slice_in_dim(flipped, first, half, 0)
        return jnp.concatenate(
            [flipped[:shared], lax.dynamic_slice_in_dim(flipped, first, half, 0)], 0
        )

    late_weights = after(weights, shards) if level > 1 else weights
    sent = with_shared(other)
    far_flipped = trade(after(sent, shards) if level > 1 else sent, level)
    far_weights = [
        trade(after(lax.dynamic_slice_in_dim(late_weights, other + a, n, 0), shards), level)
        for a, n in pieces_of(pieces)
    ]
    if shared:
        far_shared = trade(after(late_weights[:shared], shards), level)
    both = lax.all_gather(shards, "tp", axis=0, tiled=True)
    chip_sum = chip_output(weights, after(hidden, both))
    layer_out = between_chips(chip_sum).sum(0).astype(jnp.bfloat16)
    paired = interleave(with_shared(mine), far_flipped, members)
    gradient = jnp.dot(paired, both, preferred_element_type=jnp.float32)
    new_weights = arrived(jnp.zeros_like(weights), shards, ahead=0)
    returned, order = [], []
    for k, ((a, n), far) in enumerate(zip(pieces_of(pieces), far_weights)):
        if k == forward_by:
            order.append(chip_sum)
        near = lax.dynamic_slice_in_dim(weights, mine + a, n, 0)
        mean = averaged(near, arrived(far, *order), gradient[shared + a : shared + a + n])
        order = [mean]
        returned.append(trade(mean, level))
        new_weights = lax.dynamic_update_slice_in_dim(new_weights, mean, mine + a, 0)
    if shared:
        far_shared = arrived(far_shared, *order)
        mean = averaged(weights[:shared], far_shared, gradient[:shared])
        new_weights = lax.dynamic_update_slice_in_dim(new_weights, mean, 0, 0)
    returned[-1] = arrived(returned[-1], layer_out, ahead=0)
    for (a, n), mean in zip(pieces_of(pieces), returned):
        new_weights = lax.dynamic_update_slice_in_dim(new_weights, mean, other + a, 0)
    return layer_out, new_weights


def per_device(weights, hidden, cotangent, hop_index):
    hidden = with_layout_constraint(hidden, Layout(major_to_minor=(0, 1, 2)))
    branches = [
        partial(mixed_step if level in PLANS else whole_step, level) for level in range(HOP_LEVELS)
    ]
    layer_out, new_weights = lax.switch(
        hop_index[0], branches, weights[0], hidden[0], cotangent[0]
    )
    return layer_out[None], new_weights[None]


def solution(mesh):
    placed = (P("node", "tp", None), P("node", None, "tp"), P("node", "tp", None), P())
    return jax.shard_map(
        per_device,
        mesh=mesh,
        in_specs=placed,
        out_specs=(P("node", "tp", None), P("node", "tp", None)),
        check_vma=False,
    )
```

```python
from functools import partial

import jax
import jax.numpy as jnp
from jax import lax
from jax.experimental import pallas as pl
from jax.experimental.layout import Layout, with_layout_constraint
from jax.sharding import PartitionSpec as P

FF = 6912
STEP_RATE = 0.5
HOP_LEVELS = 3
SCALE = FF ** (-0.5)
CORES = 2
PLANS = {1: (128, (48, 48, 56), 1), 2: (0, (72, 72, 72), 1)}


def after(value, *others):
    return lax.optimization_barrier((value, *others))[0]


def trade(value, level):
    pairs = [(i, i ^ 1 << level) for i in range(lax.axis_size("node"))]
    return lax.ppermute(value, "node", pairs)


def swap_cores(value):
    return lax.ppermute(value, "tp", [(i, i ^ 1) for i in range(lax.axis_size("tp"))])


def between_chips(blocks):
    chips = blocks.shape[0]
    same_core = [[CORES * i + j for i in range(chips)] for j in range(CORES)]
    return lax.all_to_all(blocks, "tp", 0, 0, axis_index_groups=same_core, tiled=True)


def chip_output(weights, hidden):
    tokens, rows = hidden.shape
    members = lax.axis_size("tp")
    chips, shard = members // CORES, tokens // members
    core = lax.rem(lax.axis_index("tp"), CORES)
    panel = hidden.reshape(chips, CORES, shard, rows)

    def partial_of(owner):
        chosen = lax.dynamic_index_in_dim(panel, owner, 1, keepdims=False)
        return SCALE * jnp.dot(
            chosen.reshape(chips * shard, rows), weights, preferred_element_type=jnp.float32
        )

    far = swap_cores(partial_of(1 - core))
    return (partial_of(core) + far).reshape(chips, shard, -1)


def interleave(near, far, members):
    rows, tokens = near.shape
    blocks = (rows, members, tokens // members)
    return jnp.stack([near.reshape(blocks), far.reshape(blocks)], 2).reshape(rows, 2 * tokens)


def arrived(value, *others, ahead=10**12):
    return pl.pallas_call(
        lambda *refs: None,
        in_specs=[pl.BlockSpec(memory_space=pl.ANY)] * (1 + len(others)),
        out_specs=pl.BlockSpec(memory_space=pl.ANY),
        out_shape=jax.ShapeDtypeStruct(value.shape, value.dtype),
        input_output_aliases={0: 0},
        cost_estimate=pl.CostEstimate(flops=ahead, bytes_accessed=0, transcendentals=0),
    )(value, *others)


def averaged(near, far, gradient):
    total = near.astype(jnp.float32) + far.astype(jnp.float32)
    return (0.5 * total - (0.5 * STEP_RATE * SCALE) * gradient).astype(jnp.bfloat16)


def pieces_of(sizes):
    first = 0
    for size in sizes:
        yield first, size
        first += size


def whole_step(level, weights, hidden, cotangent):
    tokens, rows = hidden.shape
    members = lax.axis_size("tp")
    far_cotangent = trade(cotangent, level)
    far_hidden = trade(hidden, level)
    shards = jnp.concatenate([cotangent, far_cotangent], 0)
    both = lax.all_gather(shards, "tp", axis=0, tiled=True)
    chip_sum = chip_output(weights, hidden)
    far_weights = trade(weights, level)
    chip_sum = arrived(chip_sum)
    layer_out = between_chips(chip_sum).sum(0).astype(jnp.bfloat16)
    both = arrived(both, far_weights, layer_out, ahead=0)
    blocks = (members, tokens // members, rows)
    panel = jnp.stack([hidden.reshape(blocks), far_hidden.reshape(blocks)], 1)
    gradient = lax.dot_general(
        panel.reshape(2 * tokens, rows),
        both,
        (((0,), (0,)), ((), ())),
        preferred_element_type=jnp.float32,
    )
    return layer_out, averaged(weights, far_weights, gradient)


def mixed_step(level, weights, hidden, cotangent):
    members = lax.axis_size("tp")
    shared, pieces, forward_by = PLANS[level]
    half = (weights.shape[0] - shared) // 2
    upper = (lax.axis_index("node") >> level) & 1
    mine, other = shared + half * upper, shared + half * (1 - upper)
    far_cotangent = trade(cotangent, level)
    shards = jnp.concatenate([cotangent, far_cotangent], 0)
    flipped = hidden.T

    def with_shared(first):
        if not shared:
            return lax.dynamic_slice_in_dim(flipped, first, half, 0)
        return jnp.concatenate(
            [flipped[:shared], lax.dynamic_slice_in_dim(flipped, first, half, 0)], 0
        )

    late_weights = after(weights, shards) if level > 1 else weights
    sent = with_shared(other)
    far_flipped = trade(after(sent, shards) if level > 1 else sent, level)
    far_weights = [
        trade(after(lax.dynamic_slice_in_dim(late_weights, other + a, n, 0), shards), level)
        for a, n in pieces_of(pieces)
    ]
    if shared:
        far_shared = trade(after(late_weights[:shared], shards), level)
    both = lax.all_gather(shards, "tp", axis=0, tiled=True)
    chip_sum = chip_output(weights, after(hidden, both))
    layer_out = between_chips(chip_sum).sum(0).astype(jnp.bfloat16)
    paired = interleave(with_shared(mine), far_flipped, members)
    gradient = jnp.dot(paired, both, preferred_element_type=jnp.float32)
    new_weights = arrived(jnp.zeros_like(weights), shards, ahead=0)
    returned, order = [], []
    for k, ((a, n), far) in enumerate(zip(pieces_of(pieces), far_weights)):
        if k == forward_by:
            order.append(chip_sum)
        near = lax.dynamic_slice_in_dim(weights, mine + a, n, 0)
        mean = averaged(near, arrived(far, *order), gradient[shared + a : shared + a + n])
        order = [mean]
        returned.append(trade(mean, level))
        new_weights = lax.dynamic_update_slice_in_dim(new_weights, mean, mine + a, 0)
    if shared:
        far_shared = arrived(far_shared, *order)
        mean = averaged(weights[:shared], far_shared, gradient[:shared])
        new_weights = lax.dynamic_update_slice_in_dim(new_weights, mean, 0, 0)
    returned[-1] = arrived(returned[-1], layer_out, ahead=0)
    for (a, n), mean in zip(pieces_of(pieces), returned):
        new_weights = lax.dynamic_update_slice_in_dim(new_weights, mean, other + a, 0)
    return layer_out, new_weights


def per_device(weights, hidden, cotangent, hop_index):
    hidden = with_layout_constraint(hidden, Layout(major_to_minor=(0, 1, 2)))
    branches = [
        partial(mixed_step if level in PLANS else whole_step, level) for level in range(HOP_LEVELS)
    ]
    layer_out, new_weights = lax.switch(
        hop_index[0], branches, weights[0], hidden[0], cotangent[0]
    )
    return layer_out[None], new_weights[None]


def solution(mesh):
    placed = (P("node", "tp", None), P("node", None, "tp"), P("node", "tp", None), P())
    return jax.shard_map(
        per_device,
        mesh=mesh,
        in_specs=placed,
        out_specs=(P("node", "tp", None), P("node", "tp", None)),
        check_vma=False,
    )
```

```python
from functools import partial

import jax
import jax.numpy as jnp
from jax import lax
from jax.experimental import pallas as pl
from jax.experimental.layout import Layout, with_layout_constraint
from jax.sharding import PartitionSpec as P

FF = 6912
STEP_RATE = 0.5
HOP_LEVELS = 3
SCALE = FF ** (-0.5)
CORES = 2
PLANS = {1: (128, (48, 48, 56), 1), 2: (0, (72, 72, 72), 1)}


def after(value, *others):
    return lax.optimization_barrier((value, *others))[0]


def trade(value, level):
    pairs = [(i, i ^ 1 << level) for i in range(lax.axis_size("node"))]
    return lax.ppermute(value, "node", pairs)


def swap_cores(value):
    return lax.ppermute(value, "tp", [(i, i ^ 1) for i in range(lax.axis_size("tp"))])


def between_chips(blocks):
    chips = blocks.shape[0]
    same_core = [[CORES * i + j for i in range(chips)] for j in range(CORES)]
    return lax.all_to_all(blocks, "tp", 0, 0, axis_index_groups=same_core, tiled=True)


def chip_output(weights, hidden):
    tokens, rows = hidden.shape
    members = lax.axis_size("tp")
    chips, shard = members // CORES, tokens // members
    core = lax.rem(lax.axis_index("tp"), CORES)
    panel = hidden.reshape(chips, CORES, shard, rows)

    def partial_of(owner):
        chosen = lax.dynamic_index_in_dim(panel, owner, 1, keepdims=False)
        return SCALE * jnp.dot(
            chosen.reshape(chips * shard, rows), weights, preferred_element_type=jnp.float32
        )

    far = swap_cores(partial_of(1 - core))
    return (partial_of(core) + far).reshape(chips, shard, -1)


def interleave(near, far, members):
    rows, tokens = near.shape
    blocks = (rows, members, tokens // members)
    return jnp.stack([near.reshape(blocks), far.reshape(blocks)], 2).reshape(rows, 2 * tokens)


def arrived(value, *others, ahead=10**12):
    return pl.pallas_call(
        lambda *refs: None,
        in_specs=[pl.BlockSpec(memory_space=pl.ANY)] * (1 + len(others)),
        out_specs=pl.BlockSpec(memory_space=pl.ANY),
        out_shape=jax.ShapeDtypeStruct(value.shape, value.dtype),
        input_output_aliases={0: 0},
        cost_estimate=pl.CostEstimate(flops=ahead, bytes_accessed=0, transcendentals=0),
    )(value, *others)


def averaged(near, far, gradient):
    total = near.astype(jnp.float32) + far.astype(jnp.float32)
    return (0.5 * total - (0.5 * STEP_RATE * SCALE) * gradient).astype(jnp.bfloat16)


def pieces_of(sizes):
    first = 0
    for size in sizes:
        yield first, size
        first += size


def whole_step(level, weights, hidden, cotangent):
    tokens, rows = hidden.shape
    members = lax.axis_size("tp")
    far_cotangent = trade(cotangent, level)
    far_hidden = trade(hidden, level)
    shards = jnp.concatenate([cotangent, far_cotangent], 0)
    both = lax.all_gather(shards, "tp", axis=0, tiled=True)
    chip_sum = chip_output(weights, hidden)
    far_weights = trade(weights, level)
    chip_sum = arrived(chip_sum)
    layer_out = between_chips(chip_sum).sum(0).astype(jnp.bfloat16)
    both = arrived(both, far_weights, layer_out, ahead=0)
    blocks = (members, tokens // members, rows)
    panel = jnp.stack([hidden.reshape(blocks), far_hidden.reshape(blocks)], 1)
    gradient = lax.dot_general(
        panel.reshape(2 * tokens, rows),
        both,
        (((0,), (0,)), ((), ())),
        preferred_element_type=jnp.float32,
    )
    return layer_out, averaged(weights, far_weights, gradient)


def mixed_step(level, weights, hidden, cotangent):
    members = lax.axis_size("tp")
    shared, pieces, forward_by = PLANS[level]
    half = (weights.shape[0] - shared) // 2
    upper = (lax.axis_index("node") >> level) & 1
    mine, other = shared + half * upper, shared + half * (1 - upper)
    far_cotangent = trade(cotangent, level)
    shards = jnp.concatenate([cotangent, far_cotangent], 0)
    flipped = hidden.T

    def with_shared(first):
        if not shared:
            return lax.dynamic_slice_in_dim(flipped, first, half, 0)
        return jnp.concatenate(
            [flipped[:shared], lax.dynamic_slice_in_dim(flipped, first, half, 0)], 0
        )

    late_weights = after(weights, shards) if level > 1 else weights
    sent = with_shared(other)
    far_flipped = trade(after(sent, shards) if level > 1 else sent, level)
    far_weights = [
        trade(after(lax.dynamic_slice_in_dim(late_weights, other + a, n, 0), shards), level)
        for a, n in pieces_of(pieces)
    ]
    if shared:
        far_shared = trade(after(late_weights[:shared], shards), level)
    both = lax.all_gather(shards, "tp", axis=0, tiled=True)
    chip_sum = chip_output(weights, after(hidden, both))
    layer_out = between_chips(chip_sum).sum(0).astype(jnp.bfloat16)
    paired = interleave(with_shared(mine), far_flipped, members)
    gradient = jnp.dot(paired, both, preferred_element_type=jnp.float32)
    new_weights = arrived(jnp.zeros_like(weights), shards, ahead=0)
    returned, order = [], []
    for k, ((a, n), far) in enumerate(zip(pieces_of(pieces), far_weights)):
        if k == forward_by:
            order.append(chip_sum)
        near = lax.dynamic_slice_in_dim(weights, mine + a, n, 0)
        mean = averaged(near, arrived(far, *order), gradient[shared + a : shared + a + n])
        order = [mean]
        returned.append(trade(mean, level))
        new_weights = lax.dynamic_update_slice_in_dim(new_weights, mean, mine + a, 0)
    if shared:
        far_shared = arrived(far_shared, *order)
        mean = averaged(weights[:shared], far_shared, gradient[:shared])
        new_weights = lax.dynamic_update_slice_in_dim(new_weights, mean, 0, 0)
    for k in (-2, -1) if level == 1 else (-1,):
        returned[k] = arrived(returned[k], layer_out, ahead=0)
    for (a, n), mean in zip(pieces_of(pieces), returned):
        new_weights = lax.dynamic_update_slice_in_dim(new_weights, mean, other + a, 0)
    return layer_out, new_weights


def per_device(weights, hidden, cotangent, hop_index):
    hidden = with_layout_constraint(hidden, Layout(major_to_minor=(0, 1, 2)))
    branches = [
        partial(mixed_step if level in PLANS else whole_step, level) for level in range(HOP_LEVELS)
    ]
    layer_out, new_weights = lax.switch(
        hop_index[0], branches, weights[0], hidden[0], cotangent[0]
    )
    return layer_out[None], new_weights[None]


def solution(mesh):
    placed = (P("node", "tp", None), P("node", None, "tp"), P("node", "tp", None), P())
    return jax.shard_map(
        per_device,
        mesh=mesh,
        in_specs=placed,
        out_specs=(P("node", "tp", None), P("node", "tp", None)),
        check_vma=False,
    )
```
